256 devices in a mesh: outer: 32 (over z, x_lo, core), node: 8 (over y, x_hi).
Axes of the slice: x: 4 (x_hi: 2, x_lo: 2; x = x_hi * 2 + x_lo), y: 4, z: 8, core: 2. Of those that a mesh axis runs over, the one named last changes fastest.
Arguments:
- hidden: bfloat16 [65536, 8192], P(('outer', 'node')), may hold values from -8 to 8
- norm_gain: float32 [8192], replicated, may hold values from 0.1 to 1.9
- key_weight: bfloat16 [8192, 512], P('node'), may hold values from -0.027621359 to 0.027621359
- key_grad: bfloat16 [65536, 512], P(('outer', 'node')), may hold values from -8 to 8
Outputs:
- hidden_grad: bfloat16 [65536, 8192], P(('outer', 'node'))
- weight_grad: float32 [8192, 512], P(('outer', 'node'))
- gain_grad: float32 [8192], P(('outer', 'node'))
The draws below stay inside these ranges and needn't reach their ends.
All inputs are finite; a program needn't handle non-finite values.
Results may differ from the reference program's by a relative error of at most 0.0029.
Values may be sent and summed in bfloat16 or wider, within the bound.
No kernel may reach another device: no remote copies, remote signals or barrier semaphores. Data moves between devices by JAX's collectives and lax.ppermute only.
A program may use at most 128 MiB of HBM per device.

```python
import math
import jax
import jax.numpy as jnp
from jax import lax

D = 8192
TOK_DEV = 256
KW = 512
TOKENS = 65536
N_OUTER = 32
N_NODE = 8


def shared_parts(key):
    weight_key = jax.random.fold_in(key, 101)
    grad_key = jax.random.fold_in(key, 102)
    weight = jnp.clip(jax.random.normal(weight_key, (D, KW), jnp.float32), -2.5, 2.5) * D ** (-0.5)
    grads = jnp.clip(2.0 * jax.random.normal(grad_key, (TOKENS, KW), jnp.float32), -8.0, 8.0)
    return (weight, grads)


def draw_key_weight(key, part):
    weight, grads = shared_parts(key)
    return weight.astype(jnp.bfloat16)


def draw_key_grad(key, part):
    weight, grads = shared_parts(key)
    return grads.astype(jnp.bfloat16)


def draw_hidden(key, part):
    weight, grads = shared_parts(key)
    key = jax.random.fold_in(key, 3)
    sign_key = jax.random.fold_in(key, 0)
    noise_key = jax.random.fold_in(key, 2)
    pair_key = jax.random.fold_in(key, 3)
    signal = jnp.dot(grads, weight.T, precision=lax.Precision.HIGHEST) / (2.0 * math.sqrt(KW / D))
    signs = 2.0 * jax.random.randint(sign_key, (TOKENS, 1), 0, 2).astype(jnp.float32) - 1.0
    count = TOKENS // TOK_DEV
    width = D // count
    pairing = jax.random.permutation(pair_key, count)
    device_of_row = jnp.arange(TOKENS, dtype=jnp.int32) // TOK_DEV
    block_of_col = jnp.arange(D, dtype=jnp.int32) // width
    spike = jnp.where(pairing[device_of_row][:, None] == block_of_col[None, :], 4.0, 1.0)
    share = jnp.full((TOKENS, 1), 0.6, jnp.float32)
    noise = jax.random.normal(noise_key, (TOKENS, D), jnp.float32)
    mixed = signs * share * signal + jnp.sqrt(1.0 - share * share) * noise * spike
    return jnp.clip(mixed, -8.0, 8.0).astype(jnp.bfloat16)


def setup_inputs(seed: int = 0) -> dict:
    arg_keys = jax.random.split(jax.random.key(seed), 5)
    hidden = draw_hidden(jax.random.fold_in(arg_keys[4], 71), 0)
    norm_gain = jnp.clip(1.0 + 0.18 * jax.random.normal(arg_keys[1], (D,), jnp.float32), 0.1, 1.9)
    key_weight = draw_key_weight(jax.random.fold_in(arg_keys[4], 71), 0)
    key_grad = draw_key_grad(jax.random.fold_in(arg_keys[4], 71), 0)
    return dict(hidden=hidden, norm_gain=norm_gain, key_weight=key_weight, key_grad=key_grad)


def reference(hidden, norm_gain, key_weight, key_grad):
    block_rows = TOK_DEV * N_NODE
    count = TOKENS // block_rows
    hidden_blocks = hidden.reshape(count, block_rows, D)
    grad_blocks = key_grad.reshape(count, block_rows, KW)

    def advance(totals, inputs_pair):
        weight_sum, gain_sum = totals
        piece_rows, grad_rows = inputs_pair
        widened = piece_rows.astype(jnp.float32)
        inv_rms = lax.rsqrt(lax.optimization_barrier(jnp.mean(widened * widened, axis=1, keepdims=True)) + 1e-05)
        scaled = widened * inv_rms
        normed = (scaled * norm_gain).astype(jnp.bfloat16)
        weight_sum = weight_sum + jnp.dot(normed.T, grad_rows, preferred_element_type=jnp.float32)
        dnormed = jnp.dot(grad_rows, key_weight.T, preferred_element_type=jnp.float32)
        gain_sum = gain_sum + lax.optimization_barrier(jnp.sum(dnormed * scaled, axis=0))
        dscaled = dnormed * norm_gain
        result = inv_rms * (dscaled - scaled * lax.optimization_barrier(jnp.mean(dscaled * scaled, axis=1, keepdims=True)))
        return ((weight_sum, gain_sum), result.astype(jnp.bfloat16))
    start_totals = (jnp.zeros((D, KW), jnp.float32), jnp.zeros((D,), jnp.float32))
    (weight_sum, gain_sum), grads = lax.scan(advance, start_totals, (hidden_blocks, grad_blocks))
    average = 1.0 / (N_OUTER * N_NODE)
    return (grads.reshape(TOKENS, D), weight_sum * average, gain_sum * average)
```

```python
import functools

import jax
import jax.numpy as jnp
from jax import lax
from jax.experimental import pallas as pl
from jax.experimental.pallas import tpu as pltpu
from jax.sharding import Mesh
from jax.sharding import PartitionSpec as P

AXES = ("z", "xl", "core", "y", "xh")
SIZES = (8, 2, 2, 4, 2)
TOK = 256
D = 8192
KW = 512
PIECE = 256
F32 = jnp.float32
BF16 = jnp.bfloat16


def norm_kernel(core, hidden, gain, own, send, inv_out):
    mine = core[0] == 1
    wide = hidden[...].astype(F32)
    inv = lax.rsqrt(jnp.mean(wide * wide, axis=1, keepdims=True) + 1e-05)
    inv_out[...] = inv
    for pair in range(D // 512):
        low = slice(pair * 512, pair * 512 + 256)
        high = slice(pair * 512 + 256, pair * 512 + 512)
        first = (hidden[:, low].astype(F32) * inv * gain[:, low]).astype(BF16)
        second = (hidden[:, high].astype(F32) * inv * gain[:, high]).astype(BF16)
        at = slice(pair * 256, pair * 256 + 256)
        own[:, at] = jnp.where(mine, second, first)
        send[:, at] = jnp.where(mine, first, second)


def norm(core, hidden, gain):
    rows = 32
    return pl.pallas_call(
        norm_kernel,
        grid_spec=pltpu.PrefetchScalarGridSpec(
            num_scalar_prefetch=1,
            grid=(TOK // rows,),
            in_specs=[
                pl.BlockSpec((rows, D), lambda i, c: (i, 0)),
                pl.BlockSpec((1, D), lambda i, c: (0, 0)),
            ],
            out_specs=[
                pl.BlockSpec((rows, D // 2), lambda i, c: (i, 0)),
                pl.BlockSpec((rows, D // 2), lambda i, c: (i, 0)),
                pl.BlockSpec((rows, 1), lambda i, c: (i, 0)),
            ],
        ),
        out_shape=[
            jax.ShapeDtypeStruct((TOK, D // 2), BF16),
            jax.ShapeDtypeStruct((TOK, D // 2), BF16),
            jax.ShapeDtypeStruct((TOK, 1), F32),
        ],
        cost_estimate=pl.CostEstimate(flops=10 * TOK * D, bytes_accessed=4 * TOK * D, transcendentals=TOK),
        compiler_params=pltpu.CompilerParams(vmem_limit_bytes=24 << 20),
        name="norm",
    )(core, hidden, gain)


def wgrad_kernel(own, other, grad_own, grad_other, out):
    dims = (((0,), (0,)), ((), ()))
    total = lax.dot_general(own[...], grad_own[...], dims, preferred_element_type=F32)
    total += lax.dot_general(other[...], grad_other[...], dims, preferred_element_type=F32)
    out[...] = total.reshape(16, 1, 32, KW).astype(BF16)


def wgrad(own, other, grad_own, grad_other):
    return pl.pallas_call(
        wgrad_kernel,
        grid=(8,),
        in_specs=[
            pl.BlockSpec((TOK, 512), lambda i: (0, i)),
            pl.BlockSpec((TOK, 512), lambda i: (0, i)),
            pl.BlockSpec((TOK, KW), lambda i: (0, 0)),
            pl.BlockSpec((TOK, KW), lambda i: (0, 0)),
        ],
        out_specs=pl.BlockSpec((16, 1, 32, KW), lambda i: (0, i, 0, 0)),
        out_shape=jax.ShapeDtypeStruct((16, 8, 32, KW), BF16),
        cost_estimate=pl.CostEstimate(flops=2 * TOK * D * KW, bytes_accessed=9 << 20, transcendentals=0),
        compiler_params=pltpu.CompilerParams(vmem_limit_bytes=24 << 20),
        name="wgrad",
    )(own, other, grad_own, grad_other)


def hgrad_kernel(pos, hidden_any, inv_ref, grad, gain, *rest):
    weights = rest[:8]
    out_any, rows_out = rest[8:10]
    hid, wts, dsc, res, acc, sem_h, sem_w, sem_o = rest[10:]
    z, xl, core, y, xh = pos[0], pos[1], pos[2], pos[3], pos[4]
    parity = lax.rem(z, 2)
    get_h = pltpu.make_async_copy(hidden_any, hid, sem_h)
    get_h.start()
    gets = [pltpu.make_async_copy(weights[a], wts.at[a], sem_w.at[a]) for a in range(8)]
    for get in gets:
        get.start()
    inv = inv_ref[...]
    acc[...] = jnp.zeros_like(acc)
    get_h.wait()
    for a in range(8):
        gets[a].wait()
        par = lax.rem(parity + a // 4, 2)
        cor = lax.rem(core + (a // 2) % 2, 2)
        high = lax.rem(xh + a % 2, 2)

        def step(d, carry, a=a, par=par, cor=cor, high=high):
            node = lax.rem(y + d, 4) * 2 + high
            at = pl.ds(pl.multiple_of((node * 4 + par * 2 + cor) * PIECE, PIECE), PIECE)
            dn = lax.dot_general(
                grad[...], wts[a, d], (((1,), (1,)), ((), ())), preferred_element_type=F32
            )
            ds = dn * gain[:, at]
            dsc[:, at] = ds
            prod = ds * (hid[:, at].astype(F32) * inv)
            acc[...] += prod[:, :128] + prod[:, 128:]
            return carry

        lax.fori_loop(0, 4, step, 0)
    node_rows = z
    a_row = lax.rem(parity + xl, 2) * 4 + lax.rem(lax.rem(node_rows, 2) + xh, 2)
    d_row = lax.rem(node_rows // 2 - y + 4, 4)
    start = pl.multiple_of((y * 2 + xh) * 32, 32)
    rows_out[...] = wts[a_row, d_row, pl.ds(start, 32), :]
    mean = jnp.sum(acc[...], axis=1, keepdims=True) * (1.0 / D)
    factor = inv * inv * mean
    puts = []
    for b in range(8):
        at = slice(b * 1024, b * 1024 + 1024)
        res[:, at] = (dsc[:, at] * inv - hid[:, at].astype(F32) * factor).astype(BF16)
        put = pltpu.make_async_copy(res.at[:, at], out_any.at[:, at], sem_o.at[b])
        put.start()
        puts.append(put)
    for put in puts:
        put.wait()


def hgrad(pos, hidden, inv, grad, gain, weights):
    vmem = pl.BlockSpec(memory_space=pltpu.VMEM)
    hbm = pl.BlockSpec(memory_space=pl.ANY)
    return pl.pallas_call(
        hgrad_kernel,
        in_specs=[pl.BlockSpec(memory_space=pltpu.SMEM), hbm, vmem, vmem, vmem] + [hbm] * 8,
        out_specs=[hbm, vmem],
        out_shape=[
            jax.ShapeDtypeStruct((TOK, D), BF16),
            jax.ShapeDtypeStruct((32, KW), BF16),
        ],
        scratch_shapes=[
            pltpu.VMEM((TOK, D), BF16),
            pltpu.VMEM((8, 4, PIECE, KW), BF16),
            pltpu.VMEM((TOK, D), F32),
            pltpu.VMEM((TOK, D), BF16),
            pltpu.VMEM((TOK, 128), F32),
            pltpu.SemaphoreType.DMA,
            pltpu.SemaphoreType.DMA((8,)),
            pltpu.SemaphoreType.DMA((8,)),
        ],
        cost_estimate=pl.CostEstimate(flops=2 * TOK * D * KW, bytes_accessed=16 << 20, transcendentals=0),
        compiler_params=pltpu.CompilerParams(vmem_limit_bytes=40 << 20),
        name="hgrad",
    )(pos, hidden, inv, grad, gain, *weights)


def shift(a, axis, by):
    n = SIZES[AXES.index(axis)]
    return lax.ppermute(a, axis, [(i, (i + by) % n) for i in range(n)])


def cross(a):
    return lax.ppermute(
        a, ("xl", "xh"), [(l * 2 + h, (1 - l) * 2 + 1 - h) for l in range(2) for h in range(2)]
    )


def gather_weight(weight, pos):
    z, core = pos[0], pos[2]
    quarter = lax.dynamic_slice_in_dim(weight, (lax.rem(z, 2) * 2 + core) * PIECE, PIECE, 0)
    near = jnp.stack([quarter, shift(quarter, "y", -1), shift(quarter, "y", 2), shift(quarter, "y", 1)])
    far = cross(near)
    near_z = shift(near, "z", -1)
    far_z = shift(far, "z", 1)
    pairs = [near, far, near_z, far_z]
    swapped = [shift(p, "core", 1) for p in pairs]
    return [near, far, swapped[0], swapped[1], near_z, far_z, swapped[2], swapped[3]]


def shards(hidden, norm_gain, key_weight, key_grad):
    pos = jnp.stack([lax.axis_index(a) for a in AXES]).astype(jnp.int32)
    gain = norm_gain.reshape(1, D)
    grad_other = shift(key_grad, "core", 1)
    own, send, inv = norm(pos[2:3], hidden, gain)
    other = shift(send, "core", 1)
    partial = wgrad(own, other, key_grad, grad_other)
    weights = gather_weight(key_weight, pos)
    part = lax.all_to_all(partial, ("xl", "y", "xh"), 0, 0, tiled=True)
    part = jnp.sum(part.astype(F32), axis=0).astype(BF16)
    part = lax.all_to_all(part, "z", 0, 0, tiled=True)
    total = jnp.sum(part.astype(F32), axis=0)
    hidden_grad, rows = hgrad(pos, hidden, inv, key_grad, gain, weights)
    average = 1.0 / TOK
    weight_grad = total * average
    outer = pos[0] * 4 + pos[1] * 2 + pos[2]
    block = outer * 8 + pos[3] * 2 + pos[4]
    gain_rows = lax.dynamic_slice_in_dim(norm_gain, block * 32, 32, 0)
    gain_grad = jnp.sum(rows.astype(F32) * weight_grad, axis=1) / gain_rows
    return (hidden_grad, weight_grad, gain_grad)


def solution(mesh):
    fine = Mesh(mesh.devices.reshape(SIZES), AXES)
    outer, node = ("z", "xl", "core"), ("y", "xh")
    both = outer + node
    return jax.shard_map(
        shards,
        mesh=fine,
        in_specs=(P(both, None), P(), P(node, None), P(both, None)),
        out_specs=(P(both, None), P(both, None), P(both)),
        check_vma=False,
    )
```

```python
import functools

import jax
import jax.numpy as jnp
from jax import lax
from jax.experimental import pallas as pl
from jax.experimental.pallas import tpu as pltpu
from jax.sharding import Mesh
from jax.sharding import PartitionSpec as P

AXES = ("z", "xl", "core", "y", "xh")
SIZES = (8, 2, 2, 4, 2)
DEVICES = 256
TOK = 256
D = 8192
KW = 512
HALF = 256
VMEM = 56 << 20
F32 = jnp.float32
BF16 = jnp.bfloat16


def norm_kernel(pos, hidden, gain, own, send, inv_out, buf, sems):
    mine = pos[2] == 1
    rows = 32
    gets = []
    for i in range(TOK // rows):
        at = pl.ds(i * rows, rows)
        get = pltpu.make_async_copy(hidden.at[at, :], buf.at[at, :], sems.at[i])
        get.start()
        gets.append(get)
    for i in range(TOK // rows):
        gets[i].wait()
        at = slice(i * rows, i * rows + rows)
        total = jnp.zeros((rows, 256), F32)
        for k in range(D // 256):
            wide = buf[at, k * 256 : k * 256 + 256].astype(F32)
            total += wide * wide
        inv = lax.rsqrt(jnp.sum(total, axis=1, keepdims=True) * (1.0 / D) + 1e-05)
        inv_out[at, :] = inv
        for pair in range(D // 512):
            low = slice(pair * 512, pair * 512 + 256)
            high = slice(pair * 512 + 256, pair * 512 + 512)
            first = (buf[at, low].astype(F32) * inv * gain[:, low]).astype(BF16)
            second = (buf[at, high].astype(F32) * inv * gain[:, high]).astype(BF16)
            to = slice(pair * 256, pair * 256 + 256)
            own[at, to] = jnp.where(mine, second, first)
            send[at, to] = jnp.where(mine, first, second)


def norm(pos, hidden, gain):
    vmem = pl.BlockSpec(memory_space=pltpu.VMEM)
    return pl.pallas_call(
        norm_kernel,
        in_specs=[pl.BlockSpec(memory_space=pltpu.SMEM), pl.BlockSpec(memory_space=pl.ANY), vmem],
        out_specs=[vmem] * 3,
        out_shape=[
            jax.ShapeDtypeStruct((TOK, D // 2), BF16),
            jax.ShapeDtypeStruct((TOK, D // 2), BF16),
            jax.ShapeDtypeStruct((TOK, 1), F32),
        ],
        scratch_shapes=[pltpu.VMEM((TOK, D), BF16), pltpu.SemaphoreType.DMA((8,))],
        cost_estimate=pl.CostEstimate(flops=10 * TOK * D, bytes_accessed=4 * TOK * D, transcendentals=TOK),
        compiler_params=pltpu.CompilerParams(vmem_limit_bytes=55 << 20),
        name="norm",
    )(pos, hidden, gain)


def wgrad_kernel(pos, own, other, grad_own, grad_other, *refs):
    y_out, x_out, tot = refs[:4], refs[4:8], refs[8]
    xl, y, xh = pos[1], pos[3], pos[4]
    x = xh * 2 + xl
    dims = (((0,), (0,)), ((), ()))
    for i in range(8):
        at = slice(i * 512, i * 512 + 512)
        total = lax.dot_general(own[:, at], grad_own[...], dims, preferred_element_type=F32)
        total += lax.dot_general(other[:, at], grad_other[...], dims, preferred_element_type=F32)
        tot[i % 2] = total.reshape(2, 4, 2, 32, KW)
        for d in range(4):
            to_y = lax.rem(y + d, 4)
            y_out[d][i] = tot[i % 2, :, to_y, :, :, :HALF].astype(y_out[d].dtype)
            to_x = lax.rem(x + d, 4)
            x_out[d][i] = tot[i % 2, lax.rem(to_x, 2), :, to_x // 2, :, HALF:].astype(x_out[d].dtype)


def wgrad(pos, own, other, grad_own, grad_other):
    kinds = (F32, BF16, BF16, BF16)
    vmem = pl.BlockSpec(memory_space=pltpu.VMEM)
    return pl.pallas_call(
        wgrad_kernel,
        in_specs=[pl.BlockSpec(memory_space=pltpu.SMEM)] + [vmem] * 4,
        out_specs=[vmem] * 8,
        out_shape=[jax.ShapeDtypeStruct((8, 2, 2, 32, HALF), k) for k in kinds]
        + [jax.ShapeDtypeStruct((8, 4, 32, HALF), k) for k in kinds],
        scratch_shapes=[pltpu.VMEM((2, 2, 4, 2, 32, KW), F32)],
        cost_estimate=pl.CostEstimate(flops=2 * TOK * D * KW, bytes_accessed=9 << 20, transcendentals=0),
        compiler_params=pltpu.CompilerParams(vmem_limit_bytes=10 << 20),
        name="wgrad",
    )(pos, own, other, grad_own, grad_other)


def split_kernel(along_x, pos, own, near, opposite, last, *outs):
    xl, y, xh = pos[1], pos[3], pos[4]
    for d in range(4):
        if along_x:
            to_x = lax.rem(xh * 2 + xl + d, 4)
            at = (slice(None), lax.rem(to_x, 2), to_x // 2)
        else:
            at = (slice(None), lax.rem(y + d, 4))
        total = own[at] + near[at].astype(F32) + opposite[at].astype(F32) + last[at].astype(F32)
        outs[d][...] = total.astype(outs[d].dtype)


def split_sum(along_x, pos, parts):
    kinds = (F32, BF16, BF16, BF16)
    vmem = pl.BlockSpec(memory_space=pltpu.VMEM)
    return pl.pallas_call(
        functools.partial(split_kernel, along_x),
        in_specs=[pl.BlockSpec(memory_space=pltpu.SMEM)] + [vmem] * 4,
        out_specs=[vmem] * 4,
        out_shape=[jax.ShapeDtypeStruct((8, 32, HALF), k) for k in kinds],
        cost_estimate=pl.CostEstimate(flops=1 << 20, bytes_accessed=3 << 20, transcendentals=0),
        compiler_params=pltpu.CompilerParams(vmem_limit_bytes=10 << 20),
        name="split_x" if along_x else "split_y",
    )(pos, *parts)


def join_kernel(*refs):
    out = refs[8]
    for half in range(2):
        own, near, opposite, last = refs[half * 4 : half * 4 + 4]
        total = own[...] + near[...].astype(F32) + opposite[...].astype(F32) + last[...].astype(F32)
        out[:, :, half * HALF : half * HALF + HALF] = total


def join_sum(first, second):
    vmem = pl.BlockSpec(memory_space=pltpu.VMEM)
    return pl.pallas_call(
        join_kernel,
        in_specs=[vmem] * 8,
        out_specs=vmem,
        out_shape=jax.ShapeDtypeStruct((8, 32, KW), F32),
        cost_estimate=pl.CostEstimate(flops=1 << 20, bytes_accessed=2 << 20, transcendentals=0),
        compiler_params=pltpu.CompilerParams(vmem_limit_bytes=8 << 20),
        name="join",
    )(*first, *second)


def hgrad_kernel(pos, hidden, inv_ref, grad, gain, weight, out, rows_out, hid, wts, dsc, res, acc, sems):
    z, xl, core, y, xh = pos[0], pos[1], pos[2], pos[3], pos[4]
    gets = [pltpu.make_async_copy(hidden, hid, sems.at[8])]
    for b in range(8):
        to = pl.ds(b * 2, 2)
        gets.append(pltpu.make_async_copy(weight.at[to], wts.at[to], sems.at[b]))
    for get in gets:
        get.start()
    acc[...] = jnp.zeros_like(acc)
    for k in range(16):
        if k == 0:
            gets[0].wait()
        if k % 2 == 0:
            gets[1 + k // 2].wait()
        first = (k % 8) * 1024 + (k // 8) * 512
        at = slice(first, first + 512)
        dn = lax.dot_general(
            grad[...], wts[k], (((1,), (1,)), ((), ())), preferred_element_type=F32
        )
        ds = dn * gain[:, at]
        dsc[:, at] = ds
        prod = ds * hid[:, at].astype(F32)
        acc[...] += (prod[:, :128] + prod[:, 128:256]) + (prod[:, 256:384] + prod[:, 384:])
    start = pl.multiple_of(core * 256 + (y * 2 + xh) * 32, 32)
    rows_out[...] = wts[xl * 8 + z, pl.ds(start, 32), :]
    inv = inv_ref[...]
    factor = inv * inv * inv * (jnp.sum(acc[...], axis=1, keepdims=True) * (1.0 / D))
    puts = []
    for b in range(8):
        at = slice(b * 32, b * 32 + 32)
        res[at, :] = (dsc[at, :] * inv[at, :] - hid[at, :].astype(F32) * factor[at, :]).astype(BF16)
        put = pltpu.make_async_copy(res.at[pl.ds(b * 32, 32), :], out.at[pl.ds(b * 32, 32), :], sems.at[b])
        put.start()
        puts.append(put)
    for put in puts:
        put.wait()


def hgrad(pos, hidden, inv, grad, gain, weight):
    vmem = pl.BlockSpec(memory_space=pltpu.VMEM)
    hbm = pl.BlockSpec(memory_space=pl.ANY)
    return pl.pallas_call(
        hgrad_kernel,
        in_specs=[pl.BlockSpec(memory_space=pltpu.SMEM), hbm, vmem, vmem, vmem, hbm],
        out_specs=[hbm, vmem],
        out_shape=[
            jax.ShapeDtypeStruct((TOK, D), BF16),
            jax.ShapeDtypeStruct((32, KW), BF16),
        ],
        scratch_shapes=[
            pltpu.VMEM((TOK, D), BF16),
            pltpu.VMEM((16, 512, KW), BF16),
            pltpu.VMEM((TOK, D), F32),
            pltpu.VMEM((TOK, D), BF16),
            pltpu.VMEM((TOK, 128), F32),
            pltpu.SemaphoreType.DMA((9,)),
        ],
        cost_estimate=pl.CostEstimate(flops=2 * TOK * D * KW, bytes_accessed=16 << 20, transcendentals=0),
        compiler_params=pltpu.CompilerParams(vmem_limit_bytes=58 << 20),
        name="hgrad",
    )(pos, hidden, inv, grad, gain, weight)


def shift(a, axis, by):
    n = SIZES[AXES.index(axis)]
    return lax.ppermute(a, axis, [(i, (i + by) % n) for i in range(n)])


def ring_x(a, by):
    place = [(x % 2) * 2 + x // 2 for x in range(4)]
    return lax.ppermute(a, ("xl", "xh"), [(place[x], place[(x + by) % 4]) for x in range(4)])


def shift_y(a, by):
    return shift(a, "y", by)


def spread(parts, move):
    return [parts[0]] + [move(parts[d], d) for d in (1, 2, 3)]


def shards(hidden, norm_gain, key_weight, key_grad):
    pos = jnp.stack([lax.axis_index(a) for a in AXES]).astype(jnp.int32)
    core = pos[2]
    tie = lax.optimization_barrier
    gain = norm_gain.reshape(1, D)
    outer = pos[0] * 4 + pos[1] * 2 + pos[2]
    block = outer * 8 + pos[3] * 2 + pos[4]
    ungain = 1.0 / lax.dynamic_slice_in_dim(norm_gain, block * 32, 32, 0)

    piece = lax.dynamic_slice_in_dim(key_weight, core * 512, 512, 0)
    weight = lax.all_gather(piece, ("core", "y", "xh"), axis=0, tiled=False)

    grad_other = shift(key_grad, "core", 1)
    own, send, inv = norm(pos, hidden, gain)
    other = shift(send, "core", 1)
    parts = wgrad(pos, own, other, key_grad, grad_other)
    by_y, by_x = list(parts[:4]), list(parts[4:])
    for d in (1, 3):
        by_y[d], by_x[d] = shift_y(by_y[d], d), ring_x(by_x[d], d)
    by_x[2], by_y[1] = tie((by_x[2], by_y[1]))
    by_y[2], by_x[2] = shift_y(by_y[2], 2), ring_x(by_x[2], 2)
    first = spread(split_sum(True, pos, by_y), ring_x)
    second = spread(split_sum(False, pos, by_x), shift_y)
    part, inv, ungain = tie((join_sum(first, second), inv, ungain))
    part = lax.all_to_all(part, "z", 0, 0, tiled=True)
    hidden_grad, rows = hgrad(pos, hidden, inv, key_grad, gain, weight)
    rows = rows.astype(F32) * ungain[:, None]
    part, rows = tie((part, rows))
    weight_grad = jnp.sum(part, axis=0) * (1.0 / DEVICES)
    gain_grad = jnp.sum(rows * weight_grad, axis=1)
    return (hidden_grad, weight_grad, gain_grad)


def solution(mesh):
    fine = Mesh(mesh.devices.reshape(SIZES), AXES)
    outer, node = ("z", "xl", "core"), ("y", "xh")
    both = outer + node
    return jax.shard_map(
        shards,
        mesh=fine,
        in_specs=(P(both, None), P(), P(node, None), P(both, None)),
        out_specs=(P(both, None), P(both, None), P(both)),
        check_vma=False,
    )
```

```python
import functools

import jax
import jax.numpy as jnp
from jax import lax
from jax.experimental import pallas as pl
from jax.experimental.pallas import tpu as pltpu
from jax.sharding import Mesh
from jax.sharding import PartitionSpec as P

AXES = ("z", "xl", "core", "y", "xh")
SIZES = (8, 2, 2, 4, 2)
DEVICES = 256
TOK = 256
D = 8192
KW = 512
HALF = 256
VMEM = 56 << 20
F32 = jnp.float32
BF16 = jnp.bfloat16


def norm_kernel(pos, hidden, gain, grad, own, send, inv_out, buf, left, away, sems):
    mine = pos[2] == 1
    rows = 32
    gets, puts = [], []
    for i in range(TOK // rows):
        at = pl.ds(i * rows, rows)
        get = pltpu.make_async_copy(hidden.at[at, :], buf.at[at, :], sems.at[0, i])
        get.start()
        gets.append(get)
    away[:, D // 2 :] = grad[...]
    for i in range(TOK // rows):
        gets[i].wait()
        at = slice(i * rows, i * rows + rows)
        total = jnp.zeros((rows, 256), F32)
        for k in range(D // 256):
            wide = buf[at, k * 256 : k * 256 + 256].astype(F32)
            total += wide * wide
        inv = lax.rsqrt(jnp.sum(total, axis=1, keepdims=True) * (1.0 / D) + 1e-05)
        inv_out[at, :] = inv
        for pair in range(D // 512):
            low = slice(pair * 512, pair * 512 + 256)
            high = slice(pair * 512 + 256, pair * 512 + 512)
            first = (buf[at, low].astype(F32) * inv * gain[:, low]).astype(BF16)
            second = (buf[at, high].astype(F32) * inv * gain[:, high]).astype(BF16)
            to = slice(pair * 256, pair * 256 + 256)
            left[at, to] = jnp.where(mine, second, first)
            away[at, to] = jnp.where(mine, first, second)
        for k, (source, target) in enumerate(((away, send), (left, own))):
            part = pl.ds(i * rows, rows)
            put = pltpu.make_async_copy(source.at[part, :], target.at[part, :], sems.at[1 + k, i])
            put.start()
            puts.append(put)
    for put in puts:
        put.wait()


def norm(pos, hidden, gain, grad):
    vmem = pl.BlockSpec(memory_space=pltpu.VMEM)
    free = pl.BlockSpec(memory_space=pl.ANY)
    return pl.pallas_call(
        norm_kernel,
        in_specs=[pl.BlockSpec(memory_space=pltpu.SMEM), free, vmem, vmem],
        out_specs=[free, free, vmem],
        out_shape=[
            jax.ShapeDtypeStruct((TOK, D // 2), BF16),
            jax.ShapeDtypeStruct((TOK, D // 2 + KW), BF16),
            jax.ShapeDtypeStruct((TOK, 1), F32),
        ],
        scratch_shapes=[
            pltpu.VMEM((TOK, D), BF16),
            pltpu.VMEM((TOK, D // 2), BF16),
            pltpu.VMEM((TOK, D // 2 + KW), BF16),
            pltpu.SemaphoreType.DMA((3, 8)),
        ],
        cost_estimate=pl.CostEstimate(flops=10 * TOK * D, bytes_accessed=4 * TOK * D, transcendentals=TOK),
        compiler_params=pltpu.CompilerParams(vmem_limit_bytes=56 << 20),
        name="norm",
    )(pos, hidden, gain, grad)


def wgrad_kernel(pos, own, other, grad_own, *refs):
    y_out, x_out, tot = refs[:4], refs[4:8], refs[8]
    xl, y, xh = pos[1], pos[3], pos[4]
    x = xh * 2 + xl
    dims = (((0,), (0,)), ((), ()))
    for i in range(8):
        at = slice(i * 512, i * 512 + 512)
        total = lax.dot_general(own[:, at], grad_own[...], dims, preferred_element_type=F32)
        total += lax.dot_general(other[:, at], other[:, D // 2 :], dims, preferred_element_type=F32)
        tot[i % 2] = total.reshape(2, 4, 2, 32, KW)
        for d in range(4):
            to_y = lax.rem(y + d, 4)
            y_out[d][i] = tot[i % 2, :, to_y, :, :, :HALF].astype(y_out[d].dtype)
            to_x = lax.rem(x + d, 4)
            x_out[d][i] = tot[i % 2, lax.rem(to_x, 2), :, to_x // 2, :, HALF:].astype(x_out[d].dtype)


def wgrad(pos, own, other, grad_own):
    kinds = (F32, BF16, BF16, BF16)
    vmem = pl.BlockSpec(memory_space=pltpu.VMEM)
    return pl.pallas_call(
        wgrad_kernel,
        in_specs=[pl.BlockSpec(memory_space=pltpu.SMEM)] + [vmem] * 3,
        out_specs=[vmem] * 8,
        out_shape=[jax.ShapeDtypeStruct((8, 2, 2, 32, HALF), k) for k in kinds]
        + [jax.ShapeDtypeStruct((8, 4, 32, HALF), k) for k in kinds],
        scratch_shapes=[pltpu.VMEM((2, 2, 4, 2, 32, KW), F32)],
        cost_estimate=pl.CostEstimate(flops=2 * TOK * D * KW, bytes_accessed=9 << 20, transcendentals=0),
        compiler_params=pltpu.CompilerParams(vmem_limit_bytes=10 << 20),
        name="wgrad",
    )(pos, own, other, grad_own)


def split_kernel(along_x, pos, own, near, opposite, last, *outs):
    xl, y, xh = pos[1], pos[3], pos[4]
    for d in range(4):
        if along_x:
            to_x = lax.rem(xh * 2 + xl + d, 4)
            at = (slice(None), lax.rem(to_x, 2), to_x // 2)
        else:
            at = (slice(None), lax.rem(y + d, 4))
        total = own[at] + near[at].astype(F32) + opposite[at].astype(F32) + last[at].astype(F32)
        outs[d][...] = total.astype(outs[d].dtype)


def split_sum(along_x, pos, parts):
    kinds = (F32, BF16, BF16, BF16)
    vmem = pl.BlockSpec(memory_space=pltpu.VMEM)
    return pl.pallas_call(
        functools.partial(split_kernel, along_x),
        in_specs=[pl.BlockSpec(memory_space=pltpu.SMEM)] + [vmem] * 4,
        out_specs=[vmem] * 4,
        out_shape=[jax.ShapeDtypeStruct((8, 32, HALF), k) for k in kinds],
        cost_estimate=pl.CostEstimate(flops=1 << 20, bytes_accessed=3 << 20, transcendentals=0),
        compiler_params=pltpu.CompilerParams(vmem_limit_bytes=10 << 20),
        name="split_x" if along_x else "split_y",
    )(pos, *parts)


def join_kernel(*refs):
    out = refs[8]
    for half in range(2):
        own, near, opposite, last = refs[half * 4 : half * 4 + 4]
        total = own[...] + near[...].astype(F32) + opposite[...].astype(F32) + last[...].astype(F32)
        out[:, :, half * HALF : half * HALF + HALF] = total


def join_sum(first, second):
    vmem = pl.BlockSpec(memory_space=pltpu.VMEM)
    return pl.pallas_call(
        join_kernel,
        in_specs=[vmem] * 8,
        out_specs=vmem,
        out_shape=jax.ShapeDtypeStruct((8, 32, KW), F32),
        cost_estimate=pl.CostEstimate(flops=1 << 20, bytes_accessed=2 << 20, transcendentals=0),
        compiler_params=pltpu.CompilerParams(vmem_limit_bytes=8 << 20),
        name="join",
    )(*first, *second)


def hgrad_kernel(pos, hidden, inv_ref, grad, gain, ungain, weight, out, rows_out, hid, wts, dsc, res, acc, sems):
    z, xl, core, y, xh = pos[0], pos[1], pos[2], pos[3], pos[4]
    gets = []
    for b in range(8):
        at = pl.ds(b * 1024, 1024)
        gets.append(
            (
                pltpu.make_async_copy(weight.at[:, :, b], wts.at[b], sems.at[0, b]),
                pltpu.make_async_copy(hidden.at[:, at], hid.at[:, at], sems.at[1, b]),
            )
        )
        for get in gets[-1]:
            get.start()
    acc[...] = jnp.zeros_like(acc)
    for b in range(8):
        for get in gets[b]:
            get.wait()
        for k in range(4):
            at = slice(b * 1024 + k * 256, b * 1024 + k * 256 + 256)
            dn = lax.dot_general(
                grad[...],
                wts[b, k // 2, (k % 2) * 4 : (k % 2) * 4 + 4].reshape(256, KW),
                (((1,), (1,)), ((), ())),
                preferred_element_type=F32,
            )
            ds = dn * gain[:, at]
            dsc[:, at] = ds
            prod = ds * hid[:, at].astype(F32)
            acc[...] += prod[:, :128] + prod[:, 128:]
    here = y * 2 + xh
    start = pl.multiple_of(lax.rem(here, 2) * 32, 32)
    rows = wts[z, xl, core * 4 + here // 2, pl.ds(start, 32), :]
    rows_out[...] = rows.astype(F32) * ungain[...]
    inv = inv_ref[...]
    factor = inv * inv * inv * (jnp.sum(acc[...], axis=1, keepdims=True) * (1.0 / D))
    puts = []
    for b in range(8):
        rows = slice(b * 32, b * 32 + 32)
        for k in range(8):
            at = slice(k * 1024, k * 1024 + 1024)
            res[rows, at] = (dsc[rows, at] * inv[rows] - hid[rows, at].astype(F32) * factor[rows]).astype(BF16)
        part = pl.ds(b * 32, 32)
        put = pltpu.make_async_copy(res.at[part, :], out.at[part, :], sems.at[0, b])
        put.start()
        puts.append(put)
    for put in puts:
        put.wait()


def hgrad(pos, hidden, inv, grad, gain, ungain, weight):
    vmem = pl.BlockSpec(memory_space=pltpu.VMEM)
    hbm = pl.BlockSpec(memory_space=pl.ANY)
    return pl.pallas_call(
        hgrad_kernel,
        in_specs=[pl.BlockSpec(memory_space=pltpu.SMEM), hbm, vmem, vmem, vmem, vmem, hbm],
        out_specs=[hbm, vmem],
        out_shape=[
            jax.ShapeDtypeStruct((TOK, D), BF16),
            jax.ShapeDtypeStruct((32, KW), F32),
        ],
        scratch_shapes=[
            pltpu.VMEM((TOK, D), BF16),
            pltpu.VMEM((8, 2, 8, 64, KW), BF16),
            pltpu.VMEM((TOK, D), F32),
            pltpu.VMEM((TOK, D), BF16),
            pltpu.VMEM((TOK, 128), F32),
            pltpu.SemaphoreType.DMA((2, 8)),
        ],
        cost_estimate=pl.CostEstimate(flops=2 * TOK * D * KW, bytes_accessed=16 << 20, transcendentals=0),
        compiler_params=pltpu.CompilerParams(vmem_limit_bytes=58 << 20),
        name="hgrad",
    )(pos, hidden, inv, grad, gain, ungain, weight)


def shift(a, axis, by):
    n = SIZES[AXES.index(axis)]
    return lax.ppermute(a, axis, [(i, (i + by) % n) for i in range(n)])


def ring_x(a, by):
    place = [(x % 2) * 2 + x // 2 for x in range(4)]
    return lax.ppermute(a, ("xl", "xh"), [(place[x], place[(x + by) % 4]) for x in range(4)])


def shift_y(a, by):
    return shift(a, "y", by)


def spread(parts, move):
    return [parts[0]] + [move(parts[d], d) for d in (1, 2, 3)]


def shards(hidden, norm_gain, key_weight, key_grad):
    pos = jnp.stack([lax.axis_index(a) for a in AXES]).astype(jnp.int32)
    core = pos[2]
    tie = lax.optimization_barrier
    gain = norm_gain.reshape(1, D)
    outer = pos[0] * 4 + pos[1] * 2 + pos[2]
    block = outer * 8 + pos[3] * 2 + pos[4]
    ungain = 1.0 / lax.dynamic_slice_in_dim(norm_gain, block * 32, 32, 0).reshape(32, 1)

    piece = lax.dynamic_slice_in_dim(key_weight, (core * 8 + pos[0]) * 64, 64, 0)
    own, send, inv = norm(pos, hidden, gain, key_grad)
    other = shift(send, "core", 1)
    piece, inv = tie((piece, inv))
    group = lax.all_to_all(jnp.broadcast_to(piece[None], (8, 64, KW)), ("y", "xh"), 0, 0, tiled=True)
    weight = lax.all_gather(group, ("core", "z"), axis=0, tiled=False).reshape(2, 8, 8, 64, KW)
    parts = wgrad(pos, own, other, key_grad)
    by_y, by_x = list(parts[:4]), list(parts[4:])
    for d in (1, 3):
        by_y[d], by_x[d] = shift_y(by_y[d], d), ring_x(by_x[d], d)
    by_x[2], by_x[1] = tie((by_x[2], by_x[1]))
    by_y[2], by_x[2] = shift_y(by_y[2], 2), ring_x(by_x[2], 2)
    first = spread(split_sum(True, pos, by_y), ring_x)
    second = spread(split_sum(False, pos, by_x), shift_y)
    part, ungain, inv = tie((join_sum(first, second), ungain, inv))
    part = lax.all_to_all(part, "z", 0, 0, tiled=True)
    hidden_grad, rows = hgrad(pos, hidden, inv, key_grad, gain, ungain, weight)
    part, rows = tie((part, rows))
    weight_grad = jnp.sum(part, axis=0) * (1.0 / DEVICES)
    gain_grad = jnp.sum(rows * weight_grad, axis=1)
    return (hidden_grad, weight_grad, gain_grad)


def solution(mesh):
    fine = Mesh(mesh.devices.reshape(SIZES), AXES)
    outer, node = ("z", "xl", "core"), ("y", "xh")
    both = outer + node
    return jax.shard_map(
        shards,
        mesh=fine,
        in_specs=(P(both, None), P(), P(node, None), P(both, None)),
        out_specs=(P(both, None), P(both, None), P(both)),
        check_vma=False,
    )
```

```python
import functools

import jax
import jax.numpy as jnp
from jax import lax
from jax.experimental import pallas as pl
from jax.experimental.pallas import tpu as pltpu
from jax.sharding import Mesh
from jax.sharding import PartitionSpec as P

AXES = ("z", "xl", "core", "y", "xh")
SIZES = (8, 2, 2, 4, 2)
DEVICES = 256
TOK = 256
D = 8192
KW = 512
HALF = 256
VMEM = 56 << 20
F32 = jnp.float32
BF16 = jnp.bfloat16


def norm_kernel(pos, hidden, gain, grad, own, send, inv_out, buf, left, away, sems):
    mine = pos[2] == 1
    rows = 32
    gets, puts = [], []
    for i in range(TOK // rows):
        at = pl.ds(i * rows, rows)
        get = pltpu.make_async_copy(hidden.at[at, :], buf.at[at, :], sems.at[0, i])
        get.start()
        gets.append(get)
    away[:, D // 2 :] = grad[...]
    for i in range(TOK // rows):
        gets[i].wait()
        at = slice(i * rows, i * rows + rows)
        total = jnp.zeros((rows, 256), F32)
        for k in range(D // 256):
            wide = buf[at, k * 256 : k * 256 + 256].astype(F32)
            total += wide * wide
        inv = lax.rsqrt(jnp.sum(total, axis=1, keepdims=True) * (1.0 / D) + 1e-05)
        inv_out[at, :] = inv
        for pair in range(D // 512):
            low = slice(pair * 512, pair * 512 + 256)
            high = slice(pair * 512 + 256, pair * 512 + 512)
            first = (buf[at, low].astype(F32) * inv * gain[:, low]).astype(BF16)
            second = (buf[at, high].astype(F32) * inv * gain[:, high]).astype(BF16)
            to = slice(pair * 256, pair * 256 + 256)
            left[at, to] = jnp.where(mine, second, first)
            away[at, to] = jnp.where(mine, first, second)
        for k, (source, target) in enumerate(((away, send), (left, own))):
            part = pl.ds(i * rows, rows)
            put = pltpu.make_async_copy(source.at[part, :], target.at[part, :], sems.at[1 + k, i])
            put.start()
            puts.append(put)
    for put in puts:
        put.wait()


def norm(pos, hidden, gain, grad):
    vmem = pl.BlockSpec(memory_space=pltpu.VMEM)
    free = pl.BlockSpec(memory_space=pl.ANY)
    return pl.pallas_call(
        norm_kernel,
        in_specs=[pl.BlockSpec(memory_space=pltpu.SMEM), free, vmem, vmem],
        out_specs=[free, free, vmem],
        out_shape=[
            jax.ShapeDtypeStruct((TOK, D // 2), BF16),
            jax.ShapeDtypeStruct((TOK, D // 2 + KW), BF16),
            jax.ShapeDtypeStruct((TOK, 1), F32),
        ],
        scratch_shapes=[
            pltpu.VMEM((TOK, D), BF16),
            pltpu.VMEM((TOK, D // 2), BF16),
            pltpu.VMEM((TOK, D // 2 + KW), BF16),
            pltpu.SemaphoreType.DMA((3, 8)),
        ],
        cost_estimate=pl.CostEstimate(flops=10 * TOK * D, bytes_accessed=4 * TOK * D, transcendentals=TOK),
        compiler_params=pltpu.CompilerParams(vmem_limit_bytes=56 << 20),
        name="norm",
    )(pos, hidden, gain, grad)


def wgrad_kernel(pos, own, other, grad_own, *refs):
    outs, mark, staged, tot, sems = refs[:8], refs[8], refs[9:17], refs[17], refs[18]
    mark[...] = jnp.zeros_like(mark)
    xl, y, xh = pos[1], pos[3], pos[4]
    x = xh * 2 + xl
    dims = (((0,), (0,)), ((), ()))
    puts = []
    for i in range(8):
        at = slice(i * 512, i * 512 + 512)
        total = lax.dot_general(own[:, at], grad_own[...], dims, preferred_element_type=F32)
        total += lax.dot_general(other[:, at], other[:, D // 2 :], dims, preferred_element_type=F32)
        tot[i % 2] = total.reshape(2, 4, 2, 32, KW)
        for d in range(4):
            to_y = lax.rem(y + d, 4)
            staged[d][i] = tot[i % 2, :, to_y, :, :, :HALF].astype(staged[d].dtype)
            to_x = lax.rem(x + d, 4)
            staged[4 + d][i] = tot[i % 2, lax.rem(to_x, 2), :, to_x // 2, :, HALF:].astype(staged[4 + d].dtype)
        if i % 4 == 3:
            part = pl.ds(i - 3, 4)
            for k in range(8):
                put = pltpu.make_async_copy(staged[k].at[part], outs[k].at[part], sems.at[i // 4, k])
                put.start()
                puts.append(put)
    for put in puts:
        put.wait()


def wgrad(pos, own, other, grad_own):
    kinds = (F32, BF16, BF16, BF16)
    vmem = pl.BlockSpec(memory_space=pltpu.VMEM)
    shapes = [((8, 2, 2, 32, HALF), k) for k in kinds] + [((8, 4, 32, HALF), k) for k in kinds]
    return pl.pallas_call(
        wgrad_kernel,
        in_specs=[pl.BlockSpec(memory_space=pltpu.SMEM)] + [vmem] * 3,
        out_specs=[pl.BlockSpec(memory_space=pl.ANY)] * 8 + [vmem],
        out_shape=[jax.ShapeDtypeStruct(*shape) for shape in shapes] + [jax.ShapeDtypeStruct((8, 128), F32)],
        scratch_shapes=[pltpu.VMEM(*shape) for shape in shapes]
        + [pltpu.VMEM((2, 2, 4, 2, 32, KW), F32), pltpu.SemaphoreType.DMA((2, 8))],
        cost_estimate=pl.CostEstimate(flops=2 * TOK * D * KW, bytes_accessed=9 << 20, transcendentals=0),
        compiler_params=pltpu.CompilerParams(vmem_limit_bytes=58 << 20),
        name="wgrad",
    )(pos, own, other, grad_own)


def group_kernel(mark, *refs):
    out = refs[4]
    for d in range(4):
        out[2 * d : 2 * d + 2] = refs[d][...]


def group_up(mark, pieces):
    vmem = pl.BlockSpec(memory_space=pltpu.VMEM)
    return pl.pallas_call(
        group_kernel,
        in_specs=[vmem] * 5,
        out_specs=vmem,
        out_shape=jax.ShapeDtypeStruct((8, 64, KW), BF16),
        cost_estimate=pl.CostEstimate(flops=0, bytes_accessed=1 << 20, transcendentals=0),
        compiler_params=pltpu.CompilerParams(vmem_limit_bytes=4 << 20),
        name="group",
    )(mark, *pieces)


def split_kernel(along_x, pos, own, near, opposite, last, *outs):
    xl, y, xh = pos[1], pos[3], pos[4]
    for d in range(4):
        if along_x:
            to_x = lax.rem(xh * 2 + xl + d, 4)
            at = (slice(None), lax.rem(to_x, 2), to_x // 2)
        else:
            at = (slice(None), lax.rem(y + d, 4))
        total = own[at] + near[at].astype(F32) + opposite[at].astype(F32) + last[at].astype(F32)
        outs[d][...] = total.astype(outs[d].dtype)


def split_sum(along_x, pos, parts):
    kinds = (F32, BF16, BF16, BF16)
    vmem = pl.BlockSpec(memory_space=pltpu.VMEM)
    return pl.pallas_call(
        functools.partial(split_kernel, along_x),
        in_specs=[pl.BlockSpec(memory_space=pltpu.SMEM)] + [vmem] * 4,
        out_specs=[vmem] * 4,
        out_shape=[jax.ShapeDtypeStruct((8, 32, HALF), k) for k in kinds],
        cost_estimate=pl.CostEstimate(flops=1 << 20, bytes_accessed=3 << 20, transcendentals=0),
        compiler_params=pltpu.CompilerParams(vmem_limit_bytes=10 << 20),
        name="split_x" if along_x else "split_y",
    )(pos, *parts)


def join_kernel(*refs):
    out = refs[8]
    for half in range(2):
        own, near, opposite, last = refs[half * 4 : half * 4 + 4]
        total = own[...] + near[...].astype(F32) + opposite[...].astype(F32) + last[...].astype(F32)
        out[:, :, half * HALF : half * HALF + HALF] = total


def join_sum(first, second):
    vmem = pl.BlockSpec(memory_space=pltpu.VMEM)
    return pl.pallas_call(
        join_kernel,
        in_specs=[vmem] * 8,
        out_specs=vmem,
        out_shape=jax.ShapeDtypeStruct((8, 32, KW), F32),
        cost_estimate=pl.CostEstimate(flops=1 << 20, bytes_accessed=2 << 20, transcendentals=0),
        compiler_params=pltpu.CompilerParams(vmem_limit_bytes=8 << 20),
        name="join",
    )(*first, *second)


def hgrad_kernel(pos, hidden, inv_ref, grad, gain, ungain, weight, out, rows_out, hid, wts, dsc, res, acc, sems):
    z, xl, core, y, xh = pos[0], pos[1], pos[2], pos[3], pos[4]
    gets = []
    nodes = [lax.rem(y + b // 2, 4) * 2 + lax.rem(xh + b % 2, 2) for b in range(8)]
    for b in range(8):
        at = pl.ds(pl.multiple_of(nodes[b] * 1024, 1024), 1024)
        gets.append(
            (
                pltpu.make_async_copy(weight.at[:, :, b], wts.at[b], sems.at[0, b]),
                pltpu.make_async_copy(hidden.at[:, at], hid.at[:, at], sems.at[1, b]),
            )
        )
        for get in gets[-1]:
            get.start()
    acc[...] = jnp.zeros_like(acc)
    for b in range(8):
        for get in gets[b]:
            get.wait()
        for k in range(4):
            at = pl.ds(pl.multiple_of(nodes[b] * 1024 + k * 256, 256), 256)
            dn = lax.dot_general(
                grad[...],
                wts[b, k // 2, (k % 2) * 4 : (k % 2) * 4 + 4].reshape(256, KW),
                (((1,), (1,)), ((), ())),
                preferred_element_type=F32,
            )
            ds = dn * gain[:, at]
            dsc[:, at] = ds
            prod = ds * hid[:, at].astype(F32)
            acc[...] += prod[:, :128] + prod[:, 128:]
    here = y * 2 + xh
    away = lax.rem(z // 2 - y + 4, 4) * 2 + lax.rem(z + xh, 2)
    start = pl.multiple_of(lax.rem(here, 2) * 32, 32)
    rows = wts[away, xl, core * 4 + here // 2, pl.ds(start, 32), :]
    rows_out[...] = rows.astype(F32) * ungain[...]
    inv = inv_ref[...]
    factor = inv * inv * inv * (jnp.sum(acc[...], axis=1, keepdims=True) * (1.0 / D))
    puts = []
    for b in range(8):
        rows = slice(b * 32, b * 32 + 32)
        for k in range(8):
            at = slice(k * 1024, k * 1024 + 1024)
            res[rows, at] = (dsc[rows, at] * inv[rows] - hid[rows, at].astype(F32) * factor[rows]).astype(BF16)
        part = pl.ds(b * 32, 32)
        put = pltpu.make_async_copy(res.at[part, :], out.at[part, :], sems.at[0, b])
        put.start()
        puts.append(put)
    for put in puts:
        put.wait()


def hgrad(pos, hidden, inv, grad, gain, ungain, weight):
    vmem = pl.BlockSpec(memory_space=pltpu.VMEM)
    hbm = pl.BlockSpec(memory_space=pl.ANY)
    return pl.pallas_call(
        hgrad_kernel,
        in_specs=[pl.BlockSpec(memory_space=pltpu.SMEM), hbm, vmem, vmem, vmem, vmem, hbm],
        out_specs=[hbm, vmem],
        out_shape=[
            jax.ShapeDtypeStruct((TOK, D), BF16),
            jax.ShapeDtypeStruct((32, KW), F32),
        ],
        scratch_shapes=[
            pltpu.VMEM((TOK, D), BF16),
            pltpu.VMEM((8, 2, 8, 64, KW), BF16),
            pltpu.VMEM((TOK, D), F32),
            pltpu.VMEM((TOK, D), BF16),
            pltpu.VMEM((TOK, 128), F32),
            pltpu.SemaphoreType.DMA((2, 8)),
        ],
        cost_estimate=pl.CostEstimate(flops=2 * TOK * D * KW, bytes_accessed=16 << 20, transcendentals=0),
        compiler_params=pltpu.CompilerParams(vmem_limit_bytes=58 << 20),
        name="hgrad",
    )(pos, hidden, inv, grad, gain, ungain, weight)


def shift(a, axis, by):
    n = SIZES[AXES.index(axis)]
    return lax.ppermute(a, axis, [(i, (i + by) % n) for i in range(n)])


def cross(a):
    return lax.ppermute(
        a, ("xl", "xh"), [(l * 2 + h, (1 - l) * 2 + 1 - h) for l in range(2) for h in range(2)]
    )


def ring_x(a, by):
    place = [(x % 2) * 2 + x // 2 for x in range(4)]
    return lax.ppermute(a, ("xl", "xh"), [(place[x], place[(x + by) % 4]) for x in range(4)])


def shift_y(a, by):
    return shift(a, "y", by)


def spread(parts, move):
    return [parts[0]] + [move(parts[d], d) for d in (1, 2, 3)]


def shards(hidden, norm_gain, key_weight, key_grad):
    pos = jnp.stack([lax.axis_index(a) for a in AXES]).astype(jnp.int32)
    core = pos[2]
    tie = lax.optimization_barrier
    gain = norm_gain.reshape(1, D)
    outer = pos[0] * 4 + pos[1] * 2 + pos[2]
    block = outer * 8 + pos[3] * 2 + pos[4]
    ungain = 1.0 / lax.dynamic_slice_in_dim(norm_gain, block * 32, 32, 0).reshape(32, 1)

    piece = lax.dynamic_slice_in_dim(key_weight, (core * 8 + pos[0]) * 64, 64, 0)
    across = cross(piece)
    own, send, inv = norm(pos, hidden, gain, key_grad)
    other = shift(send, "core", 1)
    across, inv = tie((across, inv))
    pair = jnp.stack([piece, across])
    moved = [shift_y(pair, -d) for d in (1, 2, 3)]
    parts = wgrad(pos, own, other, key_grad)
    group = group_up(parts[8], [pair] + moved)
    weight = lax.all_gather(group, ("core", "z"), axis=0, tiled=False).reshape(2, 8, 8, 64, KW)
    by_y, by_x = list(parts[:4]), list(parts[4:8])
    for d in (1, 3):
        by_y[d], by_x[d] = shift_y(by_y[d], d), ring_x(by_x[d], d)
    by_x[2], by_x[1] = tie((by_x[2], by_x[1]))
    by_y[2], by_x[2] = shift_y(by_y[2], 2), ring_x(by_x[2], 2)
    first = spread(split_sum(True, pos, by_y), ring_x)
    second = spread(split_sum(False, pos, by_x), shift_y)
    part, ungain, inv = tie((join_sum(first, second), ungain, inv))
    part = lax.all_to_all(part, "z", 0, 0, tiled=True)
    hidden_grad, rows = hgrad(pos, hidden, inv, key_grad, gain, ungain, weight)
    part, rows = tie((part, rows))
    weight_grad = jnp.sum(part, axis=0) * (1.0 / DEVICES)
    gain_grad = jnp.sum(rows * weight_grad, axis=1)
    return (hidden_grad, weight_grad, gain_grad)


def solution(mesh):
    fine = Mesh(mesh.devices.reshape(SIZES), AXES)
    outer, node = ("z", "xl", "core"), ("y", "xh")
    both = outer + node
    return jax.shard_map(
        shards,
        mesh=fine,
        in_specs=(P(both, None), P(), P(node, None), P(both, None)),
        out_specs=(P(both, None), P(both, None), P(both)),
        check_vma=False,
    )
```

```python
import functools

import jax
import jax.numpy as jnp
from jax import lax
from jax.experimental import pallas as pl
from jax.experimental.pallas import tpu as pltpu
from jax.sharding import Mesh
from jax.sharding import PartitionSpec as P

AXES = ("z", "xl", "core", "y", "xh")
SIZES = (8, 2, 2, 4, 2)
DEVICES = 256
TOK = 256
D = 8192
KW = 512
HALF = 256
VMEM = 56 << 20
F32 = jnp.float32
BF16 = jnp.bfloat16


def norm_kernel(pos, hidden, gain, grad, own, send, inv_out, buf, left, away, sems):
    mine = pos[2] == 1
    rows = 32
    gets, puts = [], []
    for i in range(TOK // rows):
        at = pl.ds(i * rows, rows)
        get = pltpu.make_async_copy(hidden.at[at, :], buf.at[at, :], sems.at[0, i])
        get.start()
        gets.append(get)
    away[:, D // 2 :] = grad[...]
    for i in range(TOK // rows):
        gets[i].wait()
        at = slice(i * rows, i * rows + rows)
        total = jnp.zeros((rows, 256), F32)
        for k in range(D // 256):
            wide = buf[at, k * 256 : k * 256 + 256].astype(F32)
            total += wide * wide
        inv = lax.rsqrt(jnp.sum(total, axis=1, keepdims=True) * (1.0 / D) + 1e-05)
        inv_out[at, :] = inv
        for pair in range(D // 512):
            low = slice(pair * 512, pair * 512 + 256)
            high = slice(pair * 512 + 256, pair * 512 + 512)
            first = (buf[at, low].astype(F32) * inv * gain[:, low]).astype(BF16)
            second = (buf[at, high].astype(F32) * inv * gain[:, high]).astype(BF16)
            to = slice(pair * 256, pair * 256 + 256)
            left[at, to] = jnp.where(mine, second, first)
            away[at, to] = jnp.where(mine, first, second)
        for k, (source, target) in enumerate(((away, send), (left, own))):
            part = pl.ds(i * rows, rows)
            put = pltpu.make_async_copy(source.at[part, :], target.at[part, :], sems.at[1 + k, i])
            put.start()
            puts.append(put)
    for put in puts:
        put.wait()


def norm(pos, hidden, gain, grad):
    vmem = pl.BlockSpec(memory_space=pltpu.VMEM)
    free = pl.BlockSpec(memory_space=pl.ANY)
    return pl.pallas_call(
        norm_kernel,
        in_specs=[pl.BlockSpec(memory_space=pltpu.SMEM), free, vmem, vmem],
        out_specs=[free, free, vmem],
        out_shape=[
            jax.ShapeDtypeStruct((TOK, D // 2), BF16),
            jax.ShapeDtypeStruct((TOK, D // 2 + KW), BF16),
            jax.ShapeDtypeStruct((TOK, 1), F32),
        ],
        scratch_shapes=[
            pltpu.VMEM((TOK, D), BF16),
            pltpu.VMEM((TOK, D // 2), BF16),
            pltpu.VMEM((TOK, D // 2 + KW), BF16),
            pltpu.SemaphoreType.DMA((3, 8)),
        ],
        cost_estimate=pl.CostEstimate(flops=10 * TOK * D, bytes_accessed=4 * TOK * D, transcendentals=TOK),
        compiler_params=pltpu.CompilerParams(vmem_limit_bytes=56 << 20),
        name="norm",
    )(pos, hidden, gain, grad)


def wgrad_kernel(pos, own, other, grad_own, *refs):
    outs, mark, staged, tot, sems = refs[:8], refs[8], refs[9:17], refs[17], refs[18]
    mark[...] = jnp.zeros_like(mark)
    xl, y, xh = pos[1], pos[3], pos[4]
    x = xh * 2 + xl
    dims = (((0,), (0,)), ((), ()))
    puts = []
    for i in range(8):
        at = slice(i * 512, i * 512 + 512)
        total = lax.dot_general(own[:, at], grad_own[...], dims, preferred_element_type=F32)
        total += lax.dot_general(other[:, at], other[:, D // 2 :], dims, preferred_element_type=F32)
        tot[i % 2] = total.reshape(2, 4, 2, 32, KW)
        for d in range(4):
            to_y = lax.rem(y + d, 4)
            staged[d][i] = tot[i % 2, :, to_y, :, :, :HALF].astype(staged[d].dtype)
            to_x = lax.rem(x + d, 4)
            staged[4 + d][i] = tot[i % 2, lax.rem(to_x, 2), :, to_x // 2, :, HALF:].astype(staged[4 + d].dtype)
        if i % 4 == 3:
            part = pl.ds(i - 3, 4)
            for k in range(8):
                put = pltpu.make_async_copy(staged[k].at[part], outs[k].at[part], sems.at[i // 4, k])
                put.start()
                puts.append(put)
    for put in puts:
        put.wait()


def wgrad(pos, own, other, grad_own):
    kinds = (F32, BF16, BF16, BF16)
    vmem = pl.BlockSpec(memory_space=pltpu.VMEM)
    shapes = [((8, 2, 2, 32, HALF), k) for k in kinds] + [((8, 4, 32, HALF), k) for k in kinds]
    return pl.pallas_call(
        wgrad_kernel,
        in_specs=[pl.BlockSpec(memory_space=pltpu.SMEM)] + [vmem] * 3,
        out_specs=[pl.BlockSpec(memory_space=pl.ANY)] * 8 + [vmem],
        out_shape=[jax.ShapeDtypeStruct(*shape) for shape in shapes] + [jax.ShapeDtypeStruct((8, 128), F32)],
        scratch_shapes=[pltpu.VMEM(*shape) for shape in shapes]
        + [pltpu.VMEM((2, 2, 4, 2, 32, KW), F32), pltpu.SemaphoreType.DMA((2, 8))],
        cost_estimate=pl.CostEstimate(flops=2 * TOK * D * KW, bytes_accessed=9 << 20, transcendentals=0),
        compiler_params=pltpu.CompilerParams(vmem_limit_bytes=53 << 20),
        name="wgrad",
    )(pos, own, other, grad_own)


def group_kernel(mark, *refs):
    out = refs[4]
    for d in range(4):
        out[2 * d : 2 * d + 2] = refs[d][...]


def group_up(mark, pieces):
    vmem = pl.BlockSpec(memory_space=pltpu.VMEM)
    return pl.pallas_call(
        group_kernel,
        in_specs=[pl.BlockSpec(memory_space=pl.ANY)] + [vmem] * 4,
        out_specs=vmem,
        out_shape=jax.ShapeDtypeStruct((8, 64, KW), BF16),
        cost_estimate=pl.CostEstimate(flops=0, bytes_accessed=1 << 20, transcendentals=0),
        compiler_params=pltpu.CompilerParams(vmem_limit_bytes=4 << 20),
        name="group",
    )(mark, *pieces)


def split_kernel(along_x, pos, own, near, opposite, last, *outs):
    xl, y, xh = pos[1], pos[3], pos[4]
    for d in range(4):
        if along_x:
            to_x = lax.rem(xh * 2 + xl + d, 4)
            at = (slice(None), lax.rem(to_x, 2), to_x // 2)
        else:
            at = (slice(None), lax.rem(y + d, 4))
        total = own[at] + near[at].astype(F32) + opposite[at].astype(F32) + last[at].astype(F32)
        outs[d][...] = total.astype(outs[d].dtype)


def split_sum(along_x, pos, parts):
    kinds = (F32, BF16, BF16, BF16)
    vmem = pl.BlockSpec(memory_space=pltpu.VMEM)
    return pl.pallas_call(
        functools.partial(split_kernel, along_x),
        in_specs=[pl.BlockSpec(memory_space=pltpu.SMEM)] + [vmem] * 4,
        out_specs=[vmem] * 4,
        out_shape=[jax.ShapeDtypeStruct((8, 32, HALF), k) for k in kinds],
        cost_estimate=pl.CostEstimate(flops=1 << 20, bytes_accessed=3 << 20, transcendentals=0),
        compiler_params=pltpu.CompilerParams(vmem_limit_bytes=10 << 20),
        name="split_x" if along_x else "split_y",
    )(pos, *parts)


def join_kernel(*refs):
    out = refs[8]
    for half in range(2):
        own, near, opposite, last = refs[half * 4 : half * 4 + 4]
        total = own[...] + near[...].astype(F32) + opposite[...].astype(F32) + last[...].astype(F32)
        out[:, :, half * HALF : half * HALF + HALF] = total


def join_sum(first, second):
    vmem = pl.BlockSpec(memory_space=pltpu.VMEM)
    return pl.pallas_call(
        join_kernel,
        in_specs=[vmem] * 8,
        out_specs=vmem,
        out_shape=jax.ShapeDtypeStruct((8, 32, KW), F32),
        cost_estimate=pl.CostEstimate(flops=1 << 20, bytes_accessed=2 << 20, transcendentals=0),
        compiler_params=pltpu.CompilerParams(vmem_limit_bytes=8 << 20),
        name="join",
    )(*first, *second)


def hgrad_kernel(pos, hidden, inv_ref, grad, gain, ungain, weight, out, rows_out, hid, wts, dsc, res, acc, sems):
    z, xl, core, y, xh = pos[0], pos[1], pos[2], pos[3], pos[4]
    gets = []
    nodes = [lax.rem(y + b // 2, 4) * 2 + lax.rem(xh + b % 2, 2) for b in range(8)]
    for b in range(8):
        at = pl.ds(pl.multiple_of(nodes[b] * 1024, 1024), 1024)
        gets.append(
            (
                pltpu.make_async_copy(weight.at[:, :, b], wts.at[b], sems.at[0, b]),
                pltpu.make_async_copy(hidden.at[:, at], hid.at[:, at], sems.at[1, b]),
            )
        )
        for get in gets[-1]:
            get.start()
    acc[...] = jnp.zeros_like(acc)
    for b in range(8):
        for get in gets[b]:
            get.wait()
        for k in range(4):
            at = pl.ds(pl.multiple_of(nodes[b] * 1024 + k * 256, 256), 256)
            dn = lax.dot_general(
                grad[...],
                wts[b, k // 2, (k % 2) * 4 : (k % 2) * 4 + 4].reshape(256, KW),
                (((1,), (1,)), ((), ())),
                preferred_element_type=F32,
            )
            ds = dn * gain[:, at]
            dsc[:, at] = ds
            prod = ds * hid[:, at].astype(F32)
            acc[...] += prod[:, :128] + prod[:, 128:]
    here = y * 2 + xh
    away = lax.rem(z // 2 - y + 4, 4) * 2 + lax.rem(z + xh, 2)
    start = pl.multiple_of(lax.rem(here, 2) * 32, 32)
    rows = wts[away, xl, core * 4 + here // 2, pl.ds(start, 32), :]
    rows_out[...] = rows.astype(F32) * ungain[...]
    inv = inv_ref[...]
    factor = inv * inv * inv * (jnp.sum(acc[...], axis=1, keepdims=True) * (1.0 / D))
    puts = []
    for b in range(8):
        rows = slice(b * 32, b * 32 + 32)
        for k in range(8):
            at = slice(k * 1024, k * 1024 + 1024)
            res[rows, at] = (dsc[rows, at] * inv[rows] - hid[rows, at].astype(F32) * factor[rows]).astype(BF16)
        part = pl.ds(b * 32, 32)
        put = pltpu.make_async_copy(res.at[part, :], out.at[part, :], sems.at[0, b])
        put.start()
        puts.append(put)
    for put in puts:
        put.wait()


def hgrad(pos, hidden, inv, grad, gain, ungain, weight):
    vmem = pl.BlockSpec(memory_space=pltpu.VMEM)
    hbm = pl.BlockSpec(memory_space=pl.ANY)
    return pl.pallas_call(
        hgrad_kernel,
        in_specs=[pl.BlockSpec(memory_space=pltpu.SMEM), hbm, vmem, vmem, vmem, vmem, hbm],
        out_specs=[hbm, vmem],
        out_shape=[
            jax.ShapeDtypeStruct((TOK, D), BF16),
            jax.ShapeDtypeStruct((32, KW), F32),
        ],
        scratch_shapes=[
            pltpu.VMEM((TOK, D), BF16),
            pltpu.VMEM((8, 2, 8, 64, KW), BF16),
            pltpu.VMEM((TOK, D), F32),
            pltpu.VMEM((TOK, D), BF16),
            pltpu.VMEM((TOK, 128), F32),
            pltpu.SemaphoreType.DMA((2, 8)),
        ],
        cost_estimate=pl.CostEstimate(flops=2 * TOK * D * KW, bytes_accessed=16 << 20, transcendentals=0),
        compiler_params=pltpu.CompilerParams(vmem_limit_bytes=58 << 20),
        name="hgrad",
    )(pos, hidden, inv, grad, gain, ungain, weight)


def shift(a, axis, by):
    n = SIZES[AXES.index(axis)]
    return lax.ppermute(a, axis, [(i, (i + by) % n) for i in range(n)])


def cross(a):
    return lax.ppermute(
        a, ("xl", "xh"), [(l * 2 + h, (1 - l) * 2 + 1 - h) for l in range(2) for h in range(2)]
    )


def ring_x(a, by):
    place = [(x % 2) * 2 + x // 2 for x in range(4)]
    return lax.ppermute(a, ("xl", "xh"), [(place[x], place[(x + by) % 4]) for x in range(4)])


def shift_y(a, by):
    return shift(a, "y", by)


def spread(parts, move):
    return [parts[0]] + [move(parts[d], d) for d in (1, 2, 3)]


def shards(hidden, norm_gain, key_weight, key_grad):
    pos = jnp.stack([lax.axis_index(a) for a in AXES]).astype(jnp.int32)
    core = pos[2]
    tie = lax.optimization_barrier
    gain = norm_gain.reshape(1, D)
    outer = pos[0] * 4 + pos[1] * 2 + pos[2]
    block = outer * 8 + pos[3] * 2 + pos[4]
    ungain = 1.0 / lax.dynamic_slice_in_dim(norm_gain, block * 32, 32, 0).reshape(32, 1)

    piece = lax.dynamic_slice_in_dim(key_weight, (core * 8 + pos[0]) * 64, 64, 0)
    across = cross(piece)
    own, send, inv = norm(pos, hidden, gain, key_grad)
    other = shift(send, "core", 1)
    across, inv = tie((across, inv))
    pair = jnp.stack([piece, across])
    moved = [shift_y(pair, -d) for d in (1, 2, 3)]
    parts = wgrad(pos, own, other, key_grad)
    group = group_up(parts[8], [pair] + moved)
    weight = lax.all_gather(group, ("core", "z"), axis=0, tiled=False).reshape(2, 8, 8, 64, KW)
    by_y, by_x = list(parts[:4]), list(parts[4:8])
    for d in (1, 3):
        by_y[d], by_x[d] = shift_y(by_y[d], d), ring_x(by_x[d], d)
    by_x[2], by_x[1] = tie((by_x[2], by_x[1]))
    by_y[2], by_x[2] = shift_y(by_y[2], 2), ring_x(by_x[2], 2)
    first = spread(split_sum(True, pos, by_y), ring_x)
    second = spread(split_sum(False, pos, by_x), shift_y)
    part, ungain, inv = tie((join_sum(first, second), ungain, inv))
    part = lax.all_to_all(part, "z", 0, 0, tiled=True)
    hidden_grad, rows = hgrad(pos, hidden, inv, key_grad, gain, ungain, weight)
    part, rows = tie((part, rows))
    weight_grad = jnp.sum(part, axis=0) * (1.0 / DEVICES)
    gain_grad = jnp.sum(rows * weight_grad, axis=1)
    return (hidden_grad, weight_grad, gain_grad)


def solution(mesh):
    fine = Mesh(mesh.devices.reshape(SIZES), AXES)
    outer, node = ("z", "xl", "core"), ("y", "xh")
    both = outer + node
    return jax.shard_map(
        shards,
        mesh=fine,
        in_specs=(P(both, None), P(), P(node, None), P(both, None)),
        out_specs=(P(both, None), P(both, None), P(both)),
        check_vma=False,
    )
```

```python
import functools

import jax
import jax.numpy as jnp
from jax import lax
from jax.experimental import pallas as pl
from jax.experimental.pallas import tpu as pltpu
from jax.sharding import Mesh
from jax.sharding import PartitionSpec as P

AXES = ("z", "xl", "core", "y", "xh")
SIZES = (8, 2, 2, 4, 2)
DEVICES = 256
TOK = 256
D = 8192
KW = 512
HALF = 256
VMEM = 56 << 20
F32 = jnp.float32
BF16 = jnp.bfloat16


def norm_kernel(core, hidden, gain, grad, own, send, inv_out, buf, left, away, sems):
    rows = 32
    gets, puts = [], []
    for i in range(TOK // rows):
        at = pl.ds(i * rows, rows)
        get = pltpu.make_async_copy(hidden.at[at, :], buf.at[at, :], sems.at[0, i])
        get.start()
        gets.append(get)
    away[:, D // 2 :] = grad[...]
    for i in range(TOK // rows):
        gets[i].wait()
        at = slice(i * rows, i * rows + rows)
        total = jnp.zeros((rows, 256), F32)
        for k in range(D // 256):
            wide = buf[at, k * 256 : k * 256 + 256].astype(F32)
            total += wide * wide
        inv = lax.rsqrt(jnp.sum(total, axis=1, keepdims=True) * (1.0 / D) + 1e-05)
        inv_out[at, :] = inv
        base = pl.multiple_of(core[0] * 256, 256)
        flip = pl.multiple_of(256 - base, 256)
        for pair in range(D // 512):
            to = slice(pair * 256, pair * 256 + 256)
            for side, target in ((base, left), (flip, away)):
                at_col = pl.ds(pl.multiple_of(pair * 512 + side, 256), 256)
                target[at, to] = (buf[at, at_col].astype(F32) * inv * gain[:, at_col]).astype(BF16)
        for k, (source, target) in enumerate(((away, send), (left, own))):
            part = pl.ds(i * rows, rows)
            put = pltpu.make_async_copy(source.at[part, :], target.at[part, :], sems.at[1 + k, i])
            put.start()
            puts.append(put)
    for put in puts:
        put.wait()


def norm(core, hidden, gain, grad):
    vmem = pl.BlockSpec(memory_space=pltpu.VMEM)
    free = pl.BlockSpec(memory_space=pl.ANY)
    return pl.pallas_call(
        norm_kernel,
        in_specs=[pl.BlockSpec(memory_space=pltpu.SMEM), free, vmem, vmem],
        out_specs=[free, free, vmem],
        out_shape=[
            jax.ShapeDtypeStruct((TOK, D // 2), BF16),
            jax.ShapeDtypeStruct((TOK, D // 2 + KW), BF16),
            jax.ShapeDtypeStruct((TOK, 1), F32),
        ],
        scratch_shapes=[
            pltpu.VMEM((TOK, D), BF16),
            pltpu.VMEM((TOK, D // 2), BF16),
            pltpu.VMEM((TOK, D // 2 + KW), BF16),
            pltpu.SemaphoreType.DMA((3, 8)),
        ],
        cost_estimate=pl.CostEstimate(flops=10 * TOK * D, bytes_accessed=4 * TOK * D, transcendentals=TOK),
        compiler_params=pltpu.CompilerParams(vmem_limit_bytes=56 << 20),
        name="norm",
    )(core, hidden, gain, grad)


def wgrad_kernel(pos, own, other, grad_own, *refs):
    outs, mark, staged, tot, sems = refs[:8], refs[8], refs[9:17], refs[17], refs[18]
    mark[...] = jnp.zeros_like(mark)
    xl, y, xh = pos[1], pos[3], pos[4]
    x = xh * 2 + xl
    dims = (((0,), (0,)), ((), ()))
    puts = []
    for i in range(8):
        at = slice(i * 512, i * 512 + 512)
        total = lax.dot_general(own[:, at], grad_own[...], dims, preferred_element_type=F32)
        total += lax.dot_general(other[:, at], other[:, D // 2 :], dims, preferred_element_type=F32)
        tot[i % 2] = total.reshape(2, 4, 2, 32, KW)
        for d in range(4):
            to_y = lax.rem(y + d, 4)
            staged[d][i] = tot[i % 2, :, to_y, :, :, :HALF].astype(staged[d].dtype)
            to_x = lax.rem(x + d, 4)
            staged[4 + d][i] = tot[i % 2, lax.rem(to_x, 2), :, to_x // 2, :, HALF:].astype(staged[4 + d].dtype)
        if i % 4 == 3:
            part = pl.ds(i - 3, 4)
            for k in range(8):
                put = pltpu.make_async_copy(staged[k].at[part], outs[k].at[part], sems.at[i // 4, k])
                put.start()
                puts.append(put)
    for put in puts:
        put.wait()


def wgrad(pos, own, other, grad_own):
    kinds = (F32, BF16, BF16, BF16)
    vmem = pl.BlockSpec(memory_space=pltpu.VMEM)
    shapes = [((8, 2, 2, 32, HALF), k) for k in kinds] + [((8, 4, 32, HALF), k) for k in kinds]
    return pl.pallas_call(
        wgrad_kernel,
        in_specs=[pl.BlockSpec(memory_space=pltpu.SMEM)] + [vmem] * 3,
        out_specs=[pl.BlockSpec(memory_space=pl.ANY)] * 8 + [vmem],
        out_shape=[jax.ShapeDtypeStruct(*shape) for shape in shapes] + [jax.ShapeDtypeStruct((8, 128), F32)],
        scratch_shapes=[pltpu.VMEM(*shape) for shape in shapes]
        + [pltpu.VMEM((2, 2, 4, 2, 32, KW), F32), pltpu.SemaphoreType.DMA((2, 8))],
        cost_estimate=pl.CostEstimate(flops=2 * TOK * D * KW, bytes_accessed=9 << 20, transcendentals=0),
        compiler_params=pltpu.CompilerParams(vmem_limit_bytes=53 << 20),
        name="wgrad",
    )(pos, own, other, grad_own)


def group_kernel(mark, *refs):
    out = refs[4]
    for d in range(4):
        out[2 * d : 2 * d + 2] = refs[d][...]


def group_up(mark, pieces):
    vmem = pl.BlockSpec(memory_space=pltpu.VMEM)
    return pl.pallas_call(
        group_kernel,
        in_specs=[pl.BlockSpec(memory_space=pl.ANY)] + [vmem] * 4,
        out_specs=vmem,
        out_shape=jax.ShapeDtypeStruct((8, 64, KW), BF16),
        cost_estimate=pl.CostEstimate(flops=0, bytes_accessed=1 << 20, transcendentals=0),
        compiler_params=pltpu.CompilerParams(vmem_limit_bytes=4 << 20),
        name="group",
    )(mark, *pieces)


def split_kernel(along_x, pos, own, near, opposite, last, *outs):
    xl, y, xh = pos[1], pos[3], pos[4]
    for d in range(4):
        if along_x:
            to_x = lax.rem(xh * 2 + xl + d, 4)
            at = (slice(None), lax.rem(to_x, 2), to_x // 2)
        else:
            at = (slice(None), lax.rem(y + d, 4))
        total = own[at] + near[at].astype(F32) + opposite[at].astype(F32) + last[at].astype(F32)
        outs[d][...] = total.astype(outs[d].dtype)


def split_sum(along_x, pos, parts):
    kinds = (F32, BF16, BF16, BF16)
    vmem = pl.BlockSpec(memory_space=pltpu.VMEM)
    return pl.pallas_call(
        functools.partial(split_kernel, along_x),
        in_specs=[pl.BlockSpec(memory_space=pltpu.SMEM)] + [vmem] * 4,
        out_specs=[vmem] * 4,
        out_shape=[jax.ShapeDtypeStruct((8, 32, HALF), k) for k in kinds],
        cost_estimate=pl.CostEstimate(flops=1 << 20, bytes_accessed=3 << 20, transcendentals=0),
        compiler_params=pltpu.CompilerParams(vmem_limit_bytes=10 << 20),
        name="split_x" if along_x else "split_y",
    )(pos, *parts)


def join_kernel(*refs):
    out = refs[8]
    for half in range(2):
        own, near, opposite, last = refs[half * 4 : half * 4 + 4]
        total = own[...] + near[...].astype(F32) + opposite[...].astype(F32) + last[...].astype(F32)
        out[:, :, half * HALF : half * HALF + HALF] = total


def join_sum(first, second):
    vmem = pl.BlockSpec(memory_space=pltpu.VMEM)
    return pl.pallas_call(
        join_kernel,
        in_specs=[vmem] * 8,
        out_specs=vmem,
        out_shape=jax.ShapeDtypeStruct((8, 32, KW), F32),
        cost_estimate=pl.CostEstimate(flops=1 << 20, bytes_accessed=2 << 20, transcendentals=0),
        compiler_params=pltpu.CompilerParams(vmem_limit_bytes=8 << 20),
        name="join",
    )(*first, *second)


def hgrad_kernel(pos, hidden, inv_ref, grad, gain, ungain, weight, out, rows_out, hid, wts, dsc, res, acc, sems):
    z, xl, core, y, xh = pos[0], pos[1], pos[2], pos[3], pos[4]
    gets = []
    nodes = [lax.rem(y + b // 2, 4) * 2 + lax.rem(xh + b % 2, 2) for b in range(8)]
    for b in range(8):
        at = pl.ds(pl.multiple_of(nodes[b] * 1024, 1024), 1024)
        gets.append(
            (
                pltpu.make_async_copy(weight.at[:, :, b], wts.at[b], sems.at[0, b]),
                pltpu.make_async_copy(hidden.at[:, at], hid.at[:, at], sems.at[1, b]),
            )
        )
        for get in gets[-1]:
            get.start()
    acc[...] = jnp.zeros_like(acc)
    for b in range(8):
        for get in gets[b]:
            get.wait()
        for k in range(4):
            at = pl.ds(pl.multiple_of(nodes[b] * 1024 + k * 256, 256), 256)
            dn = lax.dot_general(
                grad[...],
                wts[b, k // 2, (k % 2) * 4 : (k % 2) * 4 + 4].reshape(256, KW),
                (((1,), (1,)), ((), ())),
                preferred_element_type=F32,
            )
            ds = dn * gain[:, at]
            dsc[:, at] = ds
            prod = ds * hid[:, at].astype(F32)
            acc[...] += prod[:, :128] + prod[:, 128:]
    here = y * 2 + xh
    away = lax.rem(z // 2 - y + 4, 4) * 2 + lax.rem(z + xh, 2)
    start = pl.multiple_of(lax.rem(here, 2) * 32, 32)
    rows = wts[away, xl, core * 4 + here // 2, pl.ds(start, 32), :]
    rows_out[...] = rows.astype(F32) * ungain[...]
    inv = inv_ref[...]
    factor = inv * inv * inv * (jnp.sum(acc[...], axis=1, keepdims=True) * (1.0 / D))
    puts = []
    for b in range(8):
        rows = slice(b * 32, b * 32 + 32)
        for k in range(8):
            at = slice(k * 1024, k * 1024 + 1024)
            res[rows, at] = (dsc[rows, at] * inv[rows] - hid[rows, at].astype(F32) * factor[rows]).astype(BF16)
        part = pl.ds(b * 32, 32)
        put = pltpu.make_async_copy(res.at[part, :], out.at[part, :], sems.at[0, b])
        put.start()
        puts.append(put)
    for put in puts:
        put.wait()


def hgrad(pos, hidden, inv, grad, gain, ungain, weight):
    vmem = pl.BlockSpec(memory_space=pltpu.VMEM)
    hbm = pl.BlockSpec(memory_space=pl.ANY)
    return pl.pallas_call(
        hgrad_kernel,
        in_specs=[pl.BlockSpec(memory_space=pltpu.SMEM), hbm, vmem, vmem, vmem, vmem, hbm],
        out_specs=[hbm, vmem],
        out_shape=[
            jax.ShapeDtypeStruct((TOK, D), BF16),
            jax.ShapeDtypeStruct((32, KW), F32),
        ],
        scratch_shapes=[
            pltpu.VMEM((TOK, D), BF16),
            pltpu.VMEM((8, 2, 8, 64, KW), BF16),
            pltpu.VMEM((TOK, D), F32),
            pltpu.VMEM((TOK, D), BF16),
            pltpu.VMEM((TOK, 128), F32),
            pltpu.SemaphoreType.DMA((2, 8)),
        ],
        cost_estimate=pl.CostEstimate(flops=2 * TOK * D * KW, bytes_accessed=16 << 20, transcendentals=0),
        compiler_params=pltpu.CompilerParams(vmem_limit_bytes=58 << 20),
        name="hgrad",
    )(pos, hidden, inv, grad, gain, ungain, weight)


def shift(a, axis, by):
    n = SIZES[AXES.index(axis)]
    return lax.ppermute(a, axis, [(i, (i + by) % n) for i in range(n)])


def cross(a):
    return lax.ppermute(
        a, ("xl", "xh"), [(l * 2 + h, (1 - l) * 2 + 1 - h) for l in range(2) for h in range(2)]
    )


def ring_x(a, by):
    place = [(x % 2) * 2 + x // 2 for x in range(4)]
    return lax.ppermute(a, ("xl", "xh"), [(place[x], place[(x + by) % 4]) for x in range(4)])


def shift_y(a, by):
    return shift(a, "y", by)


def spread(parts, move):
    return [parts[0]] + [move(parts[d], d) for d in (1, 2, 3)]


def shards(hidden, norm_gain, key_weight, key_grad):
    pos = jnp.stack([lax.axis_index(a) for a in AXES]).astype(jnp.int32)
    core = pos[2]
    tie = lax.optimization_barrier
    gain = norm_gain.reshape(1, D)
    outer = pos[0] * 4 + pos[1] * 2 + pos[2]
    block = outer * 8 + pos[3] * 2 + pos[4]
    ungain = 1.0 / lax.dynamic_slice_in_dim(norm_gain, block * 32, 32, 0).reshape(32, 1)

    piece = lax.dynamic_slice_in_dim(key_weight, (core * 8 + pos[0]) * 64, 64, 0)
    across = cross(piece)
    own, send, inv = norm(lax.axis_index("core").astype(jnp.int32).reshape(1), hidden, gain, key_grad)
    other = shift(send, "core", 1)
    across, inv = tie((across, inv))
    pair = jnp.stack([piece, across])
    moved = [shift_y(pair, -d) for d in (1, 2, 3)]
    parts = wgrad(pos, own, other, key_grad)
    group = group_up(parts[8], [pair] + moved)
    weight = lax.all_gather(group, ("core", "z"), axis=0, tiled=False).reshape(2, 8, 8, 64, KW)
    by_y, by_x = list(parts[:4]), list(parts[4:8])
    for d in (1, 3):
        by_y[d], by_x[d] = shift_y(by_y[d], d), ring_x(by_x[d], d)
    by_x[2], by_x[1] = tie((by_x[2], by_x[1]))
    by_y[2], by_x[2] = shift_y(by_y[2], 2), ring_x(by_x[2], 2)
    first = spread(split_sum(True, pos, by_y), ring_x)
    second = spread(split_sum(False, pos, by_x), shift_y)
    part, ungain, inv = tie((join_sum(first, second), ungain, inv))
    part = lax.all_to_all(part, "z", 0, 0, tiled=True)
    hidden_grad, rows = hgrad(pos, hidden, inv, key_grad, gain, ungain, weight)
    part, rows = tie((part, rows))
    weight_grad = jnp.sum(part, axis=0) * (1.0 / DEVICES)
    gain_grad = jnp.sum(rows * weight_grad, axis=1)
    return (hidden_grad, weight_grad, gain_grad)


def solution(mesh):
    fine = Mesh(mesh.devices.reshape(SIZES), AXES)
    outer, node = ("z", "xl", "core"), ("y", "xh")
    both = outer + node
    return jax.shard_map(
        shards,
        mesh=fine,
        in_specs=(P(both, None), P(), P(node, None), P(both, None)),
        out_specs=(P(both, None), P(both, None), P(both)),
        check_vma=False,
    )
```
